32 devices in a mesh: groups: 2 (over y), gx: 4 (over z), gy: 4 (over x, core).
Axes of the slice: x: 2, y: 2, z: 4, core: 2. Of those that a mesh axis runs over, the one named last changes fastest.
Arguments:
- velocity: float32 [3, 64, 64, 128], P(None, ('groups', 'gx'), 'gy'), parts along dimension 1, may hold values from -6 to 6
- viscosity: float32 [64, 64, 128], P(('groups', 'gx'), 'gy'), parts along dimension 0, may hold values from 0.1 to 3
- marker_force: float32 [256, 3, 128], P(('groups', 'gx', 'gy')), parts along dimension 0, may hold values from -300 to 300
- delta_weights: float32 [256, 3, 4, 128], P(('groups', 'gx', 'gy')), parts along dimension 0, may hold values from 0 to 0.5, as said below
- marker_cells: int32 [256, 3, 128], P(('groups', 'gx', 'gy')), parts along dimension 0, may hold values from 0 to 127, as said below
- block_count: int32 [256], P(('groups', 'gx', 'gy')), parts along dimension 0, may hold values from 1 to 128, as said below
- destination: int32 [256], P(('groups', 'gx', 'gy')), parts along dimension 0, may hold values from 0 to 15, as said below
Outputs:
- flow: float32 [3, 64, 64, 128], P(None, ('groups', 'gx'), 'gy'), parts along dimension 1
- marker_velocity: float32 [256, 3, 128], P(('groups', 'gx', 'gy')), parts along dimension 0
The draws below stay inside these ranges and needn't reach their ends.
There are 2 independent parts, one for each index of `groups`. The reference program is written for one: setup_inputs(seed, part) draws one part's arguments, and reference() takes and returns one part's arrays. A program takes and returns all parts, laid end to end along the dimension named above; each array names one. Nothing has to cross between parts.
Inputs may be any that keep to these rules, and one draw needn't show every extreme that they name: A block's destination is its source device or one of the eight devices at most one index away along gx and along gy, with wrap-around; the source of block k is device k // 8, and a flat index is the gx index times the size of gy plus the gy index. At most 2 blocks of one device go to one destination, every device keeps at least one of its blocks, every device sends exactly 2 to one of them, and in every draw some device receives 2 blocks from each of its nine sources. `marker_cells`: components are below 8, 16 and 128 for x, y and z. `block_count`: markers at or beyond the count are padding; their data are arbitrary. `delta_weights`: peskin four-point weights of a marker's fractional offset along each direction; the four weights of one direction sum to one.
All inputs are finite; a program needn't handle non-finite values.
Results may differ from the reference program's by a relative error of at most 0.00013.
Values sent between devices are 32-bit elements; how exact they have to be, the bound alone decides.
A program may use at most 64 MiB of HBM per device.

```python
import math
import jax
import jax.numpy as jnp
from jax import lax

CX = 8
CY = 16
NZ = 128
MB_DEV = 8
CAP = 2
MARKERS = 128
SWEEPS = 8
NX = 32
NY = 64
BLOCKS = 128
N_GX = 4
N_GY = 4


def permute_rows(base_key, rows, length):

    def one_row(row_key):
        return jax.random.permutation(row_key, length).astype(jnp.int32)
    return jax.vmap(one_row)(jax.random.split(base_key, rows))


def draw_destination(key, part):
    key = jax.random.fold_in(key, 11)
    star_key, order_key, rest_key, shuffle_key = jax.random.split(key, 4)
    device_total = N_GX * N_GY
    star = jax.random.randint(star_key, (), 0, device_total).astype(jnp.int32)
    source = jnp.arange(device_total, dtype=jnp.int32)
    source_x = source // N_GY
    source_y = source % N_GY
    toward_x = (star // N_GY - source_x + 1) % N_GX
    toward_y = (star % N_GY - source_y + 1) % N_GY
    nearby = (toward_x <= 2) & (toward_y <= 2)
    wanted = toward_x * 3 + toward_y
    order = permute_rows(order_key, device_total, 9)
    swapped = jnp.where(order == wanted[:, None], order[:, :1], order)
    swapped = swapped.at[:, 0].set(wanted)
    order = jnp.where(nearby[:, None], swapped, order)
    staying = jnp.where(order == 4, order[:, 1:2], order)
    staying = staying.at[:, 1].set(4)
    order = jnp.where((order[:, 0] != 4)[:, None], staying, order)
    rest = permute_rows(rest_key, device_total, 8 * CAP)
    rest = jnp.where(rest == 0, rest[:, :1], rest)
    rest = rest.at[:, 0].set(0)
    picked = rest[:, :MB_DEV - CAP] // CAP
    chosen_rest = jnp.take_along_axis(order[:, 1:], picked, axis=1)
    offsets_all = jnp.concatenate([jnp.repeat(order[:, :1], CAP, axis=1), chosen_rest], axis=1)
    shuffle = permute_rows(shuffle_key, device_total, MB_DEV)
    offsets_all = jnp.take_along_axis(offsets_all, shuffle, axis=1)
    move_x = offsets_all // 3 - 1
    move_y = offsets_all % 3 - 1
    target = (source_x[:, None] + move_x) % N_GX * N_GY + (source_y[:, None] + move_y) % N_GY
    return target.reshape(-1).astype(jnp.int32)


def draw_marker_cells(key, part):
    key = jax.random.fold_in(key, 12)
    first_key, second_key, third_key = jax.random.split(key, 3)
    along_x = jax.random.randint(first_key, (BLOCKS, 1, MARKERS), 0, CX)
    along_y = jax.random.randint(second_key, (BLOCKS, 1, MARKERS), 0, CY)
    along_z = jax.random.randint(third_key, (BLOCKS, 1, MARKERS), 0, NZ)
    cells = jnp.concatenate([along_x, along_y, along_z], axis=1).astype(jnp.int32)
    cells = cells.at[0, 2, 0].set(NZ - 1)
    cells = cells.at[0, :, 1].set(0)
    return cells


def draw_block_count(key, part):
    key = jax.random.fold_in(key, 13)
    counts = jax.random.randint(key, (BLOCKS,), 1, MARKERS + 1).astype(jnp.int32)
    counts = counts.at[0].set(MARKERS)
    counts = counts.at[1].set(1)
    return counts


def draw_delta_weights(key, part):
    key = jax.random.fold_in(key, 14)
    fraction = jax.random.uniform(key, (BLOCKS, 3, 1, MARKERS), jnp.float32)
    distance = jnp.abs((jnp.arange(4, dtype=jnp.float32) - 1.0)[None, None, :, None] - fraction)
    inner = (3.0 - 2.0 * distance + jnp.sqrt(jnp.maximum(1.0 + 4.0 * distance - 4.0 * distance * distance, 0.0))) / 8.0
    outer = (5.0 - 2.0 * distance - jnp.sqrt(jnp.maximum(-7.0 + 12.0 * distance - 4.0 * distance * distance, 0.0))) / 8.0
    return jnp.where(distance < 1.0, inner, jnp.where(distance < 2.0, outer, 0.0)).astype(jnp.float32)


def steps_of(key, shape, cuts, low, largest):
    def one(position, shards_of):
        steps = jax.random.uniform(jax.random.fold_in(jax.random.fold_in(key, 6), position), (shards_of,), jnp.float32, low / len(cuts), largest / len(cuts))
        return jnp.repeat(jnp.exp(steps), shape[position] // shards_of).reshape((-1,) + (1,) * (len(shape) - position - 1))

    factor_of = one(*cuts[0])
    for cut in cuts[1:]:
        factor_of = factor_of * one(*cut)
    return factor_of


def normal_values(key, extent, deviation, reach, pieces=(), kind=jnp.bfloat16):
    gain = steps_of(key, extent, pieces, -0.22, 0.18) if pieces else 1.0
    drawn = jax.random.normal(key, extent, jnp.float32) * deviation * gain
    return jnp.minimum(jnp.maximum(drawn, -reach), reach).astype(kind)


def setup_inputs(seed: int = 0, part: int = 0) -> dict:
    splits = jax.random.split(jax.random.key(seed), 8)
    own_keys = jax.random.split(jax.random.fold_in(splits[7], part), 8)
    velocity = normal_values(own_keys[0], (3, NX, NY, NZ), 1.0, 6.0, ((1, 4), (2, 4)), jnp.float32)
    viscosity = jnp.clip(jnp.exp(math.log(3.0) - 3.4011974 * jax.random.uniform(own_keys[1], (NX, NY, NZ), jnp.float32) ** steps_of(own_keys[1], (NX, NY, NZ), ((0, 4), (1, 4)), -0.2, 0.2)), 0.1, 3.0)
    marker_force = normal_values(own_keys[2], (BLOCKS, 3, MARKERS), 50.0, 300.0, ((0, 16),), jnp.float32)
    delta_weights = draw_delta_weights(jax.random.fold_in(jax.random.fold_in(splits[7], part), 71), part)
    marker_cells = draw_marker_cells(jax.random.fold_in(jax.random.fold_in(splits[7], part), 71), part)
    block_count = draw_block_count(jax.random.fold_in(jax.random.fold_in(splits[7], part), 71), part)
    destination = draw_destination(jax.random.fold_in(jax.random.fold_in(splits[7], part), 71), part)
    return dict(velocity=velocity, viscosity=viscosity, marker_force=marker_force, delta_weights=delta_weights, marker_cells=marker_cells, block_count=block_count, destination=destination)


KAPPA = 2.0


def reference(velocity, viscosity, marker_force, delta_weights, marker_cells, block_count, destination):
    size_x, size_y, size_z = viscosity.shape
    block_total = destination.shape[0]
    marker_iota = jnp.arange(MARKERS, dtype=jnp.int32)
    live_mask = (marker_iota[None, :] < block_count[:, None]).astype(jnp.float32)
    force = marker_force * live_mask[:, None, :]
    base_x = (destination // N_GY)[:, None] * CX + marker_cells[:, 0]
    base_y = (destination % N_GY)[:, None] * CY + marker_cells[:, 1]
    offsets = jnp.arange(4, dtype=jnp.int32) - 1
    cell_z = (marker_cells[:, 2][:, :, None] + offsets[None, None, :]) % size_z
    weight_z = jnp.swapaxes(delta_weights[:, 2], 1, 2)
    spread_grid = jnp.zeros((3, size_x * size_y * size_z), jnp.float32)
    stencil = []
    for offset_x in range(4):
        cell_x = (base_x + (offset_x - 1)) % size_x
        for offset_y in range(4):
            cell_y = (base_y + (offset_y - 1)) % size_y
            weight_cube = (delta_weights[:, 0, offset_x] * delta_weights[:, 1, offset_y])[:, :, None] * weight_z
            flat_index = ((cell_x * size_y + cell_y)[:, :, None] * size_z + cell_z).reshape(-1)
            values = jnp.moveaxis(force[:, :, :, None] * weight_cube[:, None], 1, 0).reshape(3, -1)
            spread_grid = spread_grid.at[:, flat_index].add(values)
            stencil.append((flat_index, weight_cube))
    source_term = velocity + spread_grid.reshape(3, size_x, size_y, size_z)
    face_east = 0.5 * (viscosity + jnp.roll(viscosity, -1, 0))
    face_west = 0.5 * (viscosity + jnp.roll(viscosity, 1, 0))
    face_north = 0.5 * (viscosity + jnp.roll(viscosity, -1, 1))
    face_south = 0.5 * (viscosity + jnp.roll(viscosity, 1, 1))
    face_up = 0.5 * (viscosity + jnp.roll(viscosity, -1, 2))
    face_down = 0.5 * (viscosity + jnp.roll(viscosity, 1, 2))
    diagonal = 1.0 + KAPPA * (face_east + face_west + face_north + face_south + face_up + face_down)
    parity = (lax.broadcasted_iota(jnp.int32, viscosity.shape, 0) + lax.broadcasted_iota(jnp.int32, viscosity.shape, 1)
              + lax.broadcasted_iota(jnp.int32, viscosity.shape, 2)) % 2
    current = velocity
    for sweep_index in range(SWEEPS):
        for colour in (0, 1):
            summed = (face_east * jnp.roll(current, -1, 1) + face_west * jnp.roll(current, 1, 1)
                      + face_north * jnp.roll(current, -1, 2) + face_south * jnp.roll(current, 1, 2)
                      + face_up * jnp.roll(current, -1, 3) + face_down * jnp.roll(current, 1, 3))
            updated = (source_term + KAPPA * summed) / diagonal
            current = jnp.where(parity == colour, updated, current)
    flattened = current.reshape(3, -1)
    gathered = jnp.zeros((3, block_total, MARKERS), jnp.float32)
    for flat_index, weight_cube in stencil:
        values = flattened[:, flat_index].reshape(3, block_total, MARKERS, 4)
        gathered = gathered + jnp.sum(values * weight_cube[None], axis=-1)
    marker_velocity = jnp.moveaxis(gathered, 0, 1) * live_mask[:, None, :]
    return current, marker_velocity
```

```python
import functools

import jax
import jax.numpy as jnp
from jax import lax
from jax.experimental import pallas as pl
from jax.experimental.pallas import tpu as pltpu
from jax.sharding import PartitionSpec as P

SWEEPS = 8
MESH = pl.DeviceIdType.MESH
F32 = jnp.float32
BF16 = jnp.bfloat16
DIRS = [(dx, dy) for dx in (-1, 0, 1) for dy in (-1, 0, 1)]
SIDES = [d for d in range(9) if d != 4]
CORNERS = [0, 2, 6, 8]
YB = 24
R0 = 9
NT = (((1,), (1,)), ((), ()))


def split(value):
    scaled = value * 65537.0
    high = scaled - (scaled - value)
    return high.astype(BF16), (value - high).astype(BF16)


def spread_reach(step, last):
    if step == 0:
        return None
    if step > 0:
        return [(last, -1), (last + 1, 0), (last + 2, 1)]
    return [(-1, last), (0, last + 1)]


def flow_reach(step, last):
    if step > 0:
        return [(last, -1)]
    return [(0, last + 1), (1, last + 2)]


def spread_corner(d, nx, ny):
    dx, dy = DIRS[d]
    rows = []
    over_x = spread_reach(dx, nx - 1) or [(-1, -1), (nx, nx)]
    over_y = spread_reach(dy, ny - 1) or [(-1, -1), (ny, ny)]
    for sx, tx in over_x:
        for sy, ty in over_y:
            if not (tx in (-1, nx) and ty in (-1, ny)):
                rows.append((sx, sy, tx, ty))
    return rows


def flow_corner(d, nx, ny):
    dx, dy = DIRS[d]
    return [
        (sx, sy, tx, ty)
        for sx, tx in flow_reach(dx, nx - 1)
        for sy, ty in flow_reach(dy, ny - 1)
    ]


def kernel(
    size_x, size_y,
    vel, visc, force, weights, cells, count, dest,
    flow, mvel,
    S, V, C, inv, src, G, fld_hi, fld_lo, fld, packed,
    mk_tx, mk_rx, mk_s, mk_r,
    vx_rx, vy_tx, vy_rx, vc_tx, vc_rx, v_s, v_r,
    sx_tx, sx_rx, sy_tx, sy_rx, sc_tx, sc_rx, st_s, st_r,
    gxp_rx, gxm_rx, gyp_tx, gyp_rx, gym_tx, gym_rx, gc_tx, gc_rx, g_s, g_r,
    fxp_rx, fxm_rx, fyp_tx, fyp_rx, fym_tx, fym_rx, fc_tx, fc_rx, f_s, f_r,
    ret_tx, ret_rx, ret_s, ret_r,
):
    nx, ny, nz = visc.shape
    blocks, markers = force.shape[0], force.shape[2]
    here_x = lax.axis_index("gx")
    here_y = lax.axis_index("gy")

    def at(d, sign=1):
        dx, dy = DIRS[d]
        return {
            "gx": lax.rem(here_x + (sign * dx + size_x), size_x),
            "gy": lax.rem(here_y + (sign * dy + size_y), size_y),
        }

    def copy(a, b, s, r, d, sign=1):
        return pltpu.make_async_remote_copy(
            src_ref=a, dst_ref=b, send_sem=s, recv_sem=r,
            device_id=at(d, sign), device_id_type=MESH,
        )

    barrier = pltpu.get_barrier_semaphore()
    for d in SIDES:
        pl.semaphore_signal(barrier, inc=1, device_id=at(d), device_id_type=MESH)

    lane = lax.broadcasted_iota(jnp.int32, (1, markers), 1)
    for b in range(blocks):
        live = lane < count[b]
        packed[b, 0:3] = jnp.where(live, force[b], 0.0)
        for k in range(3):
            packed[b, 3 + 4 * k:7 + 4 * k] = jnp.where(live, weights[b, k], 0.0)
        packed[b, 15:18] = jnp.where(live, cells[b].astype(F32), 0.0)
        packed[b, 18:24] = jnp.zeros((6, markers), F32)
    going, rank = [], []
    for b in range(blocks):
        to = dest[b]
        step_x = lax.rem(lax.div(to, size_y) - here_x + (1 + size_x), size_x)
        step_y = lax.rem(lax.rem(to, size_y) - here_y + (1 + size_y), size_y)
        going.append(step_x * 3 + step_y)
        r = jnp.int32(0)
        for e in range(b):
            r = r + (going[e] == going[b]).astype(jnp.int32)
        rank.append(r)
    slot_of = [going[b] * 2 + rank[b] for b in range(blocks)]
    for d in range(9):
        for k in range(2):
            which, valid = jnp.int32(0), jnp.int32(0)
            for b in range(blocks):
                hit = (slot_of[b] == d * 2 + k).astype(jnp.int32)
                which, valid = which + b * hit, valid + hit
            block = packed[which] * valid.astype(F32)
            if d == 4:
                mk_rx[d, k] = block
            else:
                mk_tx[d, k] = block

    pl.semaphore_wait(barrier, 8)
    mk = {d: copy(mk_tx.at[d], mk_rx.at[d], mk_s.at[d], mk_r.at[d], d) for d in SIDES}
    for d in SIDES:
        mk[d].start()

    for i, lo in ((0, 0), (1, ny - 2)):
        for k in range(2):
            vy_tx[i, k] = visc[:, lo + k, :]
    for i, d in enumerate(CORNERS):
        dx, dy = DIRS[d]
        x, y = (nx - 1 if dx > 0 else 0), (ny - 1 if dy > 0 else 0)
        vc_tx[i] = visc[x, y:y + 1, :]
    vcopies = [
        copy(visc.at[0:2], vx_rx.at[0], v_s.at[1], v_r.at[1], 1),
        copy(visc.at[nx - 2:nx], vx_rx.at[1], v_s.at[7], v_r.at[7], 7),
        copy(vy_tx.at[0], vy_rx.at[0], v_s.at[3], v_r.at[3], 3),
        copy(vy_tx.at[1], vy_rx.at[1], v_s.at[5], v_r.at[5], 5),
    ] + [
        copy(vc_tx.at[i], vc_rx.at[i], v_s.at[d], v_r.at[d], d) for i, d in enumerate(CORNERS)
    ]
    for c in vcopies:
        c.start()

    S[...] = jnp.zeros(S.shape, F32)
    V[...] = jnp.zeros(V.shape, F32)
    for c in range(3):
        S[c, 2:2 + nx, R0:R0 + ny, :] = vel[c]
    odd = (
        lax.broadcasted_iota(jnp.int32, (ny, nz), 0) + lax.broadcasted_iota(jnp.int32, (ny, nz), 1)
    ) % 2 == 1
    odd_x = (
        lax.broadcasted_iota(jnp.int32, (nx, nz), 0) + lax.broadcasted_iota(jnp.int32, (nx, nz), 1)
    ) % 2 == 1

    def state_copies(slot):
        out = [
            copy(sx_tx.at[slot, i], sx_rx.at[slot, i], st_s.at[slot, d], st_r.at[slot, d], d)
            for i, d in ((0, 1), (1, 7))
        ]
        out += [
            copy(sy_tx.at[slot, i], sy_rx.at[slot, i], st_s.at[slot, d], st_r.at[slot, d], d)
            for i, d in ((0, 3), (1, 5))
        ]
        out += [
            copy(sc_tx.at[slot, i], sc_rx.at[slot, i], st_s.at[slot, d], st_r.at[slot, d], d)
            for i, d in enumerate(CORNERS)
        ]
        return out

    def send_state(slot):
        for c in range(3):
            for i, x in ((0, 0), (1, nx - 2)):
                sx_tx[slot, i, c] = jnp.where(
                    odd, S[c, 2 + x, R0:R0 + ny, :], S[c, 3 + x, R0:R0 + ny, :]
                )
            for i, y in ((0, 0), (1, ny - 2)):
                sy_tx[slot, i, c] = jnp.where(
                    odd_x, S[c, 2:2 + nx, R0 + y, :], S[c, 2:2 + nx, R0 + y + 1, :]
                )
            for i, d in enumerate(CORNERS):
                dx, dy = DIRS[d]
                x, y = (nx - 1 if dx > 0 else 0), (ny - 1 if dy > 0 else 0)
                sc_tx[slot, i, c] = S[c, 2 + x, R0 + y:R0 + y + 1, :]
        for c in state_copies(slot):
            c.start()

    def take_state(slot):
        for c in state_copies(slot):
            c.wait()
        for c in range(3):
            for i, x in ((0, nx), (1, -2)):
                plane = sx_rx[slot, i, c]
                S[c, 2 + x, R0:R0 + ny, :] = plane
                S[c, 3 + x, R0:R0 + ny, :] = plane
            for i, y in ((0, ny), (1, -2)):
                tile = sy_rx[slot, i, c]
                S[c, 2:2 + nx, R0 + y, :] = tile
                S[c, 2:2 + nx, R0 + y + 1, :] = tile
            for i, d in enumerate(CORNERS):
                dx, dy = DIRS[d]
                x, y = (-1 if dx > 0 else nx), (-1 if dy > 0 else ny)
                S[c, 2 + x, R0 + y:R0 + y + 1, :] = sc_rx[slot, i, c]

    send_state(0)

    V[2:2 + nx, R0:R0 + ny, :] = visc[...]
    for c in vcopies:
        c.wait()
    for i, x in ((0, nx), (1, -2)):
        V[2 + x:4 + x, R0:R0 + ny, :] = vx_rx[i]
    for i, y in ((0, ny), (1, -2)):
        for k in range(2):
            V[2:2 + nx, R0 + y + k, :] = vy_rx[i, k]
    for i, d in enumerate(CORNERS):
        dx, dy = DIRS[d]
        x, y = (-1 if dx > 0 else nx), (-1 if dy > 0 else ny)
        V[2 + x, R0 + y:R0 + y + 1, :] = vc_rx[i]
    lo, hi = R0 - 1, R0 - 1 + 24

    def coefficient(i, carry):
        mid = V[i + 1, lo:hi, :]
        around = [
            V[i + 2, lo:hi, :],
            V[i, lo:hi, :],
            V[i + 1, lo + 1:hi + 1, :],
            V[i + 1, lo - 1:hi - 1, :],
            pltpu.roll(mid, nz - 1, 1),
            pltpu.roll(mid, 1, 1),
        ]
        faces = [mid + a for a in around]
        total = faces[0]
        for f in faces[1:]:
            total = total + f
        recip = 1.0 / (1.0 + total)
        inv[i] = recip
        for k in range(6):
            C[k, i] = faces[k] * recip
        return carry

    lax.fori_loop(0, nx + 2, coefficient, 0)

    row_x = lax.broadcasted_iota(jnp.int32, (16, markers), 0)
    row_y = lax.broadcasted_iota(jnp.int32, (YB, markers), 0)
    row_z = lax.broadcasted_iota(jnp.int32, (nz, markers), 0)

    def tables(blk):
        place = blk[15:18].astype(jnp.int32)
        tx = jnp.zeros((16, markers), F32)
        ty = jnp.zeros((YB, markers), F32)
        tz = jnp.zeros((nz, markers), F32)
        for o in range(4):
            px = place[0:1] + o
            py = place[1:2] + (o - 1)
            py = jnp.where(py < 0, py + YB, py)
            pz = (place[2:3] + (o - 1 + nz)) % nz
            tx = jnp.where(row_x == px, blk[3 + o:4 + o], tx)
            ty = jnp.where(row_y == py, blk[7 + o:8 + o], ty)
            tz = jnp.where(row_z == pz, blk[11 + o:12 + o], tz)
        txy = jnp.concatenate([tx[i:i + 1] * ty for i in range(nx + 4)], axis=0)
        return txy, tz

    G[...] = jnp.zeros(G.shape, F32)
    for c in range(3):
        G[1:1 + nx, 0:ny, c * nz:(c + 1) * nz] = vel[c]
    for d in SIDES:
        mk[d].wait()

    def dot(a, b, dims):
        return lax.dot_general(a, b, dims, preferred_element_type=F32)

    def spread(d, carry):
        left, right = [], []
        for k in range(2):
            blk = mk_rx[d, k]
            txy, tz = tables(blk)
            left.append(txy)
            right.append(jnp.concatenate([tz * blk[c:c + 1] for c in range(3)], axis=0))
        left_hi, left_lo = split(jnp.concatenate(left, axis=1))
        right_hi, right_lo = split(jnp.concatenate(right, axis=1))
        got = dot(left_hi, right_hi, NT) + dot(left_hi, right_lo, NT) + dot(left_lo, right_hi, NT)
        G[...] += got.reshape(G.shape)
        return carry

    lax.fori_loop(0, 9, spread, 0)

    def g_row(y):
        return y % YB

    for k, (y, _) in enumerate(spread_reach(1, ny - 1)):
        gyp_tx[k] = G[1:1 + nx, g_row(y), :]
    for k, (y, _) in enumerate(spread_reach(-1, ny - 1)):
        gym_tx[k] = G[1:1 + nx, g_row(y), :]
    for i, d in enumerate(SIDES):
        for k, (sx, sy, _, _) in enumerate(spread_corner(d, nx, ny)):
            gc_tx[i, k] = G[sx + 1, g_row(sy):g_row(sy) + 1, :]
    gcopies = [
        copy(G.at[nx:nx + 3, 0:ny], gxp_rx, g_s.at[7], g_r.at[7], 7),
        copy(G.at[0:2, 0:ny], gxm_rx, g_s.at[1], g_r.at[1], 1),
        copy(gyp_tx, gyp_rx, g_s.at[5], g_r.at[5], 5),
        copy(gym_tx, gym_rx, g_s.at[3], g_r.at[3], 3),
    ]
    for i, d in enumerate(SIDES):
        n = len(spread_corner(d, nx, ny))
        gcopies.append(copy(gc_tx.at[i, 0:n], gc_rx.at[i, 0:n], g_s.at[9 + i], g_r.at[9 + i], d))
    for c in gcopies:
        c.start()
    src[...] = jnp.zeros(src.shape, F32)
    for c in range(3):
        z = slice(c * nz, (c + 1) * nz)
        src[c, :, 1:2 + ny, :] = G[0:nx + 2, 0:ny + 1, z]
        src[c, :, 0:1, :] = G[0:nx + 2, YB - 1:YB, z]
    for c in gcopies:
        c.wait()
    for c in range(3):
        z = slice(c * nz, (c + 1) * nz)
        src[c, 0:3, 1:1 + ny, :] += gxp_rx[:, :, z]
        src[c, nx:nx + 2, 1:1 + ny, :] += gxm_rx[:, :, z]
        for k, (_, y) in enumerate(spread_reach(1, ny - 1)):
            src[c, 1:1 + nx, 1 + y, :] += gyp_rx[k, :, z]
        for k, (_, y) in enumerate(spread_reach(-1, ny - 1)):
            src[c, 1:1 + nx, 1 + y, :] += gym_rx[k, :, z]
        for i, d in enumerate(SIDES):
            for k, (_, _, x, y) in enumerate(spread_corner(d, nx, ny)):
                src[c, 1 + x, 1 + y:2 + y, :] += gc_rx[i, k, :, z]
        src[c] = src[c] * inv[...]

    def update(first, last, low, high, colour):
        rows = high - low
        parity = (
            lax.broadcasted_iota(jnp.int32, (rows, nz), 0)
            + lax.broadcasted_iota(jnp.int32, (rows, nz), 1)
            + low
        ) % 2
        a, b = R0 + low, R0 + high
        p, q = 1 + low, 1 + high
        for x in range(first, last):
            chosen = parity == (colour + x) % 2
            coef = [C[k, x + 1, p:q, :] for k in range(6)]
            for c in range(3):
                mid = S[c, x + 2, a:b, :]
                new = (
                    src[c, x + 1, p:q, :]
                    + coef[0] * S[c, x + 3, a:b, :]
                    + coef[1] * S[c, x + 1, a:b, :]
                    + coef[2] * S[c, x + 2, a + 1:b + 1, :]
                    + coef[3] * S[c, x + 2, a - 1:b - 1, :]
                    + coef[4] * pltpu.roll(mid, nz - 1, 1)
                    + coef[5] * pltpu.roll(mid, 1, 1)
                )
                S[c, x + 2, a:b, :] = jnp.where(chosen, new, mid)

    def sweep(r, carry):
        take_state(lax.rem(r, 2))
        update(-1, nx + 1, -1, 23, 0)
        update(0, nx, 0, ny, 1)

        @pl.when(r < SWEEPS - 1)
        def _():
            send_state(lax.rem(r + 1, 2))

        return carry

    lax.fori_loop(0, SWEEPS, sweep, 0)

    for c in range(3):
        flow[c] = S[c, 2:2 + nx, R0:R0 + ny, :]
        for k, (y, _) in enumerate(flow_reach(1, ny - 1)):
            fyp_tx[k, c] = S[c, 2:2 + nx, R0 + y, :]
        for k, (y, _) in enumerate(flow_reach(-1, ny - 1)):
            fym_tx[k, c] = S[c, 2:2 + nx, R0 + y, :]
        for i, d in enumerate(CORNERS):
            for k, (sx, sy, _, _) in enumerate(flow_corner(d, nx, ny)):
                fc_tx[i, 3 * k + c] = S[c, 2 + sx, R0 + sy:R0 + sy + 1, :]
    fcopies = [
        copy(flow.at[:, nx - 1:nx], fxp_rx, f_s.at[7], f_r.at[7], 7),
        copy(flow.at[:, 0:2], fxm_rx, f_s.at[1], f_r.at[1], 1),
        copy(fyp_tx, fyp_rx, f_s.at[5], f_r.at[5], 5),
        copy(fym_tx, fym_rx, f_s.at[3], f_r.at[3], 3),
    ]
    for i, d in enumerate(CORNERS):
        n = 3 * len(flow_corner(d, nx, ny))
        fcopies.append(copy(fc_tx.at[i, 0:n], fc_rx.at[i, 0:n], f_s.at[d], f_r.at[d], d))
    for c in fcopies:
        c.start()
    fld[...] = jnp.zeros(fld.shape, F32)
    for c in range(3):
        fld[c, 1:1 + nx, 0:ny, :] = S[c, 2:2 + nx, R0:R0 + ny, :]
    for c in fcopies:
        c.wait()
    fld[:, 0:1, 0:ny, :] = fxp_rx[...]
    fld[:, 1 + nx:3 + nx, 0:ny, :] = fxm_rx[...]
    for c in range(3):
        for k, (_, y) in enumerate(flow_reach(1, ny - 1)):
            fld[c, 1:1 + nx, g_row(y), :] = fyp_rx[k, c]
        for k, (_, y) in enumerate(flow_reach(-1, ny - 1)):
            fld[c, 1:1 + nx, g_row(y), :] = fym_rx[k, c]
        for i, d in enumerate(CORNERS):
            for k, (_, _, x, y) in enumerate(flow_corner(d, nx, ny)):
                fld[c, 1 + x, g_row(y):g_row(y) + 1, :] = fc_rx[i, 3 * k + c]
    high, low = split(fld[...].reshape(-1, nz))
    fld_hi[...] = high
    fld_lo[...] = low
    NN = (((1,), (0,)), ((), ()))

    def sample(d, carry):
        pairs = [tables(mk_rx[d, k]) for k in range(2)]
        txy = jnp.concatenate([p[0] for p in pairs], axis=1)
        tz_hi, tz_lo = split(jnp.concatenate([p[1] for p in pairs], axis=1))
        picked = dot(fld_hi[...], tz_hi, NN) + dot(fld_lo[...], tz_hi, NN) + dot(fld_hi[...], tz_lo, NN)
        rows = txy.shape[0]
        for c in range(3):
            total = jnp.sum(picked[c * rows:(c + 1) * rows] * txy, axis=0, keepdims=True)
            ret_tx[d, 0, c:c + 1] = total[:, :markers]
            ret_tx[d, 1, c:c + 1] = total[:, markers:]
        return carry

    ret_tx[...] = jnp.zeros(ret_tx.shape, F32)
    lax.fori_loop(0, 9, sample, 0)
    back = [copy(ret_tx.at[d], ret_rx.at[d], ret_s.at[d], ret_r.at[d], d, -1) for d in SIDES]
    for c in back:
        c.start()
    ret_rx[4] = ret_tx[4]
    for c in back:
        c.wait()
    for b in range(blocks):
        mvel[b] = ret_rx[jnp.clip(going[b], 0, 8), jnp.clip(rank[b], 0, 1)][0:3]


def local(velocity, viscosity, marker_force, delta_weights, marker_cells, block_count, destination):
    nx, ny, nz = viscosity.shape
    size_x, size_y = lax.axis_size("gx"), lax.axis_size("gy")
    blocks, _, markers = marker_force.shape
    dma = pltpu.SemaphoreType.DMA
    vmem = pltpu.VMEM
    rows = 3 * (nx + 4) * YB
    scratch = [
        vmem((3, nx + 4, 40, nz), F32),
        vmem((nx + 4, 40, nz), F32),
        vmem((6, nx + 2, 24, nz), F32),
        vmem((nx + 2, 24, nz), F32),
        vmem((3, nx + 2, 24, nz), F32),
        vmem((nx + 4, YB, 3 * nz), F32),
        vmem((rows, nz), BF16),
        vmem((rows, nz), BF16),
        vmem((3, nx + 4, YB, nz), F32),
        vmem((blocks, 24, markers), F32),
        vmem((9, 2, 24, markers), F32), vmem((9, 2, 24, markers), F32), dma((9,)), dma((9,)),
        vmem((2, 2, ny, nz), F32),
        vmem((2, 2, nx, nz), F32), vmem((2, 2, nx, nz), F32),
        vmem((4, 1, nz), F32), vmem((4, 1, nz), F32), dma((9,)), dma((9,)),
        vmem((2, 2, 3, ny, nz), F32), vmem((2, 2, 3, ny, nz), F32),
        vmem((2, 2, 3, nx, nz), F32), vmem((2, 2, 3, nx, nz), F32),
        vmem((2, 4, 3, 1, nz), F32), vmem((2, 4, 3, 1, nz), F32), dma((2, 9)), dma((2, 9)),
        vmem((3, ny, 3 * nz), F32), vmem((2, ny, 3 * nz), F32),
        vmem((3, nx, 3 * nz), F32), vmem((3, nx, 3 * nz), F32),
        vmem((2, nx, 3 * nz), F32), vmem((2, nx, 3 * nz), F32),
        vmem((8, 8, 1, 3 * nz), F32), vmem((8, 8, 1, 3 * nz), F32), dma((17,)), dma((17,)),
        vmem((3, 1, ny, nz), F32), vmem((3, 2, ny, nz), F32),
        vmem((1, 3, nx, nz), F32), vmem((1, 3, nx, nz), F32),
        vmem((2, 3, nx, nz), F32), vmem((2, 3, nx, nz), F32),
        vmem((4, 12, 1, nz), F32), vmem((4, 12, 1, nz), F32), dma((9,)), dma((9,)),
        vmem((9, 2, 8, markers), F32), vmem((9, 2, 8, markers), F32), dma((9,)), dma((9,)),
    ]
    in_vmem = pl.BlockSpec(memory_space=pltpu.VMEM)
    in_smem = pl.BlockSpec(memory_space=pltpu.SMEM)
    return pl.pallas_call(
        functools.partial(kernel, size_x, size_y),
        out_shape=(
            jax.ShapeDtypeStruct(velocity.shape, F32),
            jax.ShapeDtypeStruct(marker_force.shape, F32),
        ),
        in_specs=[in_vmem] * 5 + [in_smem] * 2,
        out_specs=(in_vmem, in_vmem),
        scratch_shapes=scratch,
        compiler_params=pltpu.CompilerParams(
            collective_id=0, has_side_effects=True, vmem_limit_bytes=40 * 1024 * 1024
        ),
    )(velocity, viscosity, marker_force, delta_weights, marker_cells, block_count, destination)


def solution(mesh):
    return jax.shard_map(
        local,
        mesh=mesh,
        in_specs=(
            P(None, ("groups", "gx"), "gy", None),
            P(("groups", "gx"), "gy", None),
            P(("groups", "gx", "gy"), None, None),
            P(("groups", "gx", "gy"), None, None, None),
            P(("groups", "gx", "gy"), None, None),
            P(("groups", "gx", "gy")),
            P(("groups", "gx", "gy")),
        ),
        out_specs=(P(None, ("groups", "gx"), "gy", None), P(("groups", "gx", "gy"), None, None)),
        check_vma=False,
    )
```

```python
import functools

import jax
import jax.numpy as jnp
from jax import lax
from jax.experimental import pallas as pl
from jax.experimental.pallas import tpu as pltpu
from jax.sharding import PartitionSpec as P

SWEEPS = 8
MESH = pl.DeviceIdType.MESH
F32 = jnp.float32
BF16 = jnp.bfloat16
DIRS = [(dx, dy) for dx in (-1, 0, 1) for dy in (-1, 0, 1)]
SIDES = [d for d in range(9) if d != 4]
CORNERS = [0, 2, 6, 8]
YB = 24
R0 = 9
NT = (((1,), (1,)), ((), ()))


def split(value):
    scaled = value * 65537.0
    high = scaled - (scaled - value)
    return high.astype(BF16), (value - high).astype(BF16)


def spread_reach(step, last):
    if step == 0:
        return None
    if step > 0:
        return [(last, -1), (last + 1, 0), (last + 2, 1)]
    return [(-1, last), (0, last + 1)]


def flow_reach(step, last):
    if step > 0:
        return [(last, -1)]
    return [(0, last + 1), (1, last + 2)]


def spread_corner(d, nx, ny):
    dx, dy = DIRS[d]
    rows = []
    over_x = spread_reach(dx, nx - 1) or [(-1, -1), (nx, nx)]
    over_y = spread_reach(dy, ny - 1) or [(-1, -1), (ny, ny)]
    for sx, tx in over_x:
        for sy, ty in over_y:
            if not (tx in (-1, nx) and ty in (-1, ny)):
                rows.append((sx, sy, tx, ty))
    return rows


def flow_corner(d, nx, ny):
    dx, dy = DIRS[d]
    return [
        (sx, sy, tx, ty)
        for sx, tx in flow_reach(dx, nx - 1)
        for sy, ty in flow_reach(dy, ny - 1)
    ]


def kernel(
    size_x, size_y,
    vel, visc, force, weights, cells, count, dest,
    flow, mvel,
    S, V, C, inv, src, G, fld_hi, fld_lo, fld, packed,
    mk_tx, mk_rx, mk_s, mk_r,
    vx_rx, vy_tx, vy_rx, vc_tx, vc_rx, v_s, v_r,
    sx_tx, sx_rx, sy_tx, sy_rx, sc_tx, sc_rx, st_s, st_r,
    gxp_rx, gxm_rx, gyp_tx, gyp_rx, gym_tx, gym_rx, gc_tx, gc_rx, g_s, g_r,
    fxp_rx, fxm_rx, fyp_tx, fyp_rx, fym_tx, fym_rx, fc_tx, fc_rx, f_s, f_r,
    ret_tx, ret_rx, ret_s, ret_r,
):
    nx, ny, nz = visc.shape
    blocks, markers = force.shape[0], force.shape[2]
    here_x = lax.axis_index("gx")
    here_y = lax.axis_index("gy")

    def at(d, sign=1):
        dx, dy = DIRS[d] if isinstance(d, int) else (d // 3 - 1, d % 3 - 1)
        return {
            "gx": lax.rem(here_x + (sign * dx + size_x), size_x),
            "gy": lax.rem(here_y + (sign * dy + size_y), size_y),
        }

    def copy(a, b, s, r, d, sign=1):
        return pltpu.make_async_remote_copy(
            src_ref=a, dst_ref=b, send_sem=s, recv_sem=r,
            device_id=at(d, sign), device_id_type=MESH,
        )

    barrier = pltpu.get_barrier_semaphore()
    for d in SIDES:
        pl.semaphore_signal(barrier, inc=1, device_id=at(d), device_id_type=MESH)

    lane = lax.broadcasted_iota(jnp.int32, (1, markers), 1)
    for b in range(blocks):
        live = lane < count[b]
        packed[b, 0:3] = jnp.where(live, force[b], 0.0)
        for k in range(3):
            packed[b, 3 + 4 * k:7 + 4 * k] = jnp.where(live, weights[b, k], 0.0)
        packed[b, 15:18] = jnp.where(live, cells[b].astype(F32), 0.0)
        packed[b, 18:24] = jnp.zeros((6, markers), F32)
    going, rank = [], []
    for b in range(blocks):
        to = dest[b]
        step_x = lax.rem(lax.div(to, size_y) - here_x + (1 + size_x), size_x)
        step_y = lax.rem(lax.rem(to, size_y) - here_y + (1 + size_y), size_y)
        going.append(step_x * 3 + step_y)
        r = jnp.int32(0)
        for e in range(b):
            r = r + (going[e] == going[b]).astype(jnp.int32)
        rank.append(r)
    slot_of = [going[b] * 2 + rank[b] for b in range(blocks)]
    for d in range(9):
        for k in range(2):
            which, valid = jnp.int32(0), jnp.int32(0)
            for b in range(blocks):
                hit = (slot_of[b] == d * 2 + k).astype(jnp.int32)
                which, valid = which + b * hit, valid + hit
            block = packed[which] * valid.astype(F32)
            if d == 4:
                mk_rx[d, k] = block
            else:
                mk_tx[d, k] = block

    pl.semaphore_wait(barrier, 8)
    mk = {d: copy(mk_tx.at[d], mk_rx.at[d], mk_s.at[d], mk_r.at[d], d) for d in SIDES}
    for d in SIDES:
        mk[d].start()

    for i, lo in ((0, 0), (1, ny - 2)):
        for k in range(2):
            vy_tx[i, k] = visc[:, lo + k, :]
    for i, d in enumerate(CORNERS):
        dx, dy = DIRS[d]
        x, y = (nx - 1 if dx > 0 else 0), (ny - 1 if dy > 0 else 0)
        vc_tx[i] = visc[x, y:y + 1, :]
    vcopies = [
        copy(visc.at[0:2], vx_rx.at[0], v_s.at[1], v_r.at[1], 1),
        copy(visc.at[nx - 2:nx], vx_rx.at[1], v_s.at[7], v_r.at[7], 7),
        copy(vy_tx.at[0], vy_rx.at[0], v_s.at[3], v_r.at[3], 3),
        copy(vy_tx.at[1], vy_rx.at[1], v_s.at[5], v_r.at[5], 5),
    ] + [
        copy(vc_tx.at[i], vc_rx.at[i], v_s.at[d], v_r.at[d], d) for i, d in enumerate(CORNERS)
    ]
    for c in vcopies:
        c.start()

    S[...] = jnp.zeros(S.shape, F32)
    for c in range(3):
        S[c, 2:2 + nx, R0:R0 + ny, :] = vel[c]
    odd = (
        lax.broadcasted_iota(jnp.int32, (ny, nz), 0) + lax.broadcasted_iota(jnp.int32, (ny, nz), 1)
    ) % 2 == 1
    odd_x = (
        lax.broadcasted_iota(jnp.int32, (nx, nz), 0) + lax.broadcasted_iota(jnp.int32, (nx, nz), 1)
    ) % 2 == 1

    def corner_cell(d):
        dx, dy = DIRS[d]
        return (nx - 1 if dx > 0 else 0), (ny - 1 if dy > 0 else 0)

    def copies_x(slot):
        return [
            copy(sx_tx.at[slot, i], sx_rx.at[slot, i], st_s.at[slot, d], st_r.at[slot, d], d)
            for i, d in ((0, 1), (1, 7))
        ] + [
            copy(sc_tx.at[slot, i], sc_rx.at[slot, i], st_s.at[slot, d], st_r.at[slot, d], d)
            for i, d in enumerate(CORNERS)
        ]

    def copies_y(slot):
        return [
            copy(sy_tx.at[slot, i], sy_rx.at[slot, i], st_s.at[slot, d], st_r.at[slot, d], d)
            for i, d in ((0, 3), (1, 5))
        ]

    def send_x(slot):
        sends = copies_x(slot)
        for i, x in ((0, 0), (1, nx - 2)):
            for c in range(3):
                sx_tx[slot, i, c] = jnp.where(
                    odd, S[c, 2 + x, R0:R0 + ny, :], S[c, 3 + x, R0:R0 + ny, :]
                )
            sends[i].start()
        for i, d in enumerate(CORNERS):
            x, y = corner_cell(d)
            for c in range(3):
                sc_tx[slot, i, c] = S[c, 2 + x, R0 + y:R0 + y + 1, :]
            sends[2 + i].start()

    def send_y(slot):
        sends = copies_y(slot)
        for i, y in ((0, 0), (1, ny - 2)):
            for c in range(3):
                sy_tx[slot, i, c] = jnp.where(
                    odd_x, S[c, 2:2 + nx, R0 + y, :], S[c, 2:2 + nx, R0 + y + 1, :]
                )
            sends[i].start()

    def take_y(slot):
        for c in copies_y(slot):
            c.wait()
        for c in range(3):
            for i, y in ((0, ny), (1, -2)):
                tile = sy_rx[slot, i, c]
                S[c, 2:2 + nx, R0 + y, :] = tile
                S[c, 2:2 + nx, R0 + y + 1, :] = tile

    def take_x(slot):
        for c in copies_x(slot):
            c.wait()
        for c in range(3):
            for i, x in ((0, nx), (1, -2)):
                plane = sx_rx[slot, i, c]
                S[c, 2 + x, R0:R0 + ny, :] = plane
                S[c, 3 + x, R0:R0 + ny, :] = plane
            for i, d in enumerate(CORNERS):
                dx, dy = DIRS[d]
                x, y = (-1 if dx > 0 else nx), (-1 if dy > 0 else ny)
                S[c, 2 + x, R0 + y:R0 + y + 1, :] = sc_rx[slot, i, c]

    send_x(0)
    send_y(0)

    row_x = lax.broadcasted_iota(jnp.int32, (16, markers), 0)
    row_y = lax.broadcasted_iota(jnp.int32, (YB, markers), 0)
    row_z = lax.broadcasted_iota(jnp.int32, (nz, markers), 0)

    def tables(blk):
        place = blk[15:18].astype(jnp.int32)
        tx = jnp.zeros((16, markers), F32)
        ty = jnp.zeros((YB, markers), F32)
        tz = jnp.zeros((nz, markers), F32)
        for o in range(4):
            px = place[0:1] + o
            py = place[1:2] + (o - 1)
            py = jnp.where(py < 0, py + YB, py)
            pz = (place[2:3] + (o - 1 + nz)) % nz
            tx = jnp.where(row_x == px, blk[3 + o:4 + o], tx)
            ty = jnp.where(row_y == py, blk[7 + o:8 + o], ty)
            tz = jnp.where(row_z == pz, blk[11 + o:12 + o], tz)
        txy = jnp.concatenate([tx[i:i + 1] * ty for i in range(nx + 4)], axis=0)
        return txy, tz

    G[...] = jnp.zeros(G.shape, F32)
    for c in range(3):
        G[1:1 + nx, 0:ny, c * nz:(c + 1) * nz] = vel[c]
    def dot(a, b, dims):
        return lax.dot_general(a, b, dims, preferred_element_type=F32)

    def spread(d, carry):
        left, right = [], []
        for k in range(2):
            blk = mk_rx[d, k]
            txy, tz = tables(blk)
            left.append(txy)
            right.append(jnp.concatenate([tz * blk[c:c + 1] for c in range(3)], axis=0))
        left_hi, left_lo = split(jnp.concatenate(left, axis=1))
        right_hi, right_lo = split(jnp.concatenate(right, axis=1))
        got = dot(left_hi, right_hi, NT) + dot(left_hi, right_lo, NT) + dot(left_lo, right_hi, NT)
        G[...] += got.reshape(G.shape)
        return carry

    lax.fori_loop(4, 5, spread, 0)
    for d in SIDES:
        mk[d].wait()
    lax.fori_loop(0, 4, spread, 0)
    lax.fori_loop(5, 9, spread, 0)

    def g_row(y):
        return y % YB

    for k, (y, _) in enumerate(spread_reach(1, ny - 1)):
        gyp_tx[k] = G[1:1 + nx, g_row(y), :]
    for k, (y, _) in enumerate(spread_reach(-1, ny - 1)):
        gym_tx[k] = G[1:1 + nx, g_row(y), :]
    for i, d in enumerate(SIDES):
        for k, (sx, sy, _, _) in enumerate(spread_corner(d, nx, ny)):
            gc_tx[i, k] = G[sx + 1, g_row(sy):g_row(sy) + 1, :]
    gcopies = [
        copy(G.at[nx:nx + 3, 0:ny], gxp_rx, g_s.at[7], g_r.at[7], 7),
        copy(G.at[0:2, 0:ny], gxm_rx, g_s.at[1], g_r.at[1], 1),
        copy(gyp_tx, gyp_rx, g_s.at[5], g_r.at[5], 5),
        copy(gym_tx, gym_rx, g_s.at[3], g_r.at[3], 3),
    ]
    for i, d in enumerate(SIDES):
        n = len(spread_corner(d, nx, ny))
        gcopies.append(copy(gc_tx.at[i, 0:n], gc_rx.at[i, 0:n], g_s.at[9 + i], g_r.at[9 + i], d))
    for c in gcopies:
        c.start()
    V[...] = jnp.zeros(V.shape, F32)
    V[2:2 + nx, R0:R0 + ny, :] = visc[...]
    for c in vcopies:
        c.wait()
    for i, x in ((0, nx), (1, -2)):
        V[2 + x:4 + x, R0:R0 + ny, :] = vx_rx[i]
    for i, y in ((0, ny), (1, -2)):
        for k in range(2):
            V[2:2 + nx, R0 + y + k, :] = vy_rx[i, k]
    for i, d in enumerate(CORNERS):
        dx, dy = DIRS[d]
        x, y = (-1 if dx > 0 else nx), (-1 if dy > 0 else ny)
        V[2 + x, R0 + y:R0 + y + 1, :] = vc_rx[i]
    lo, hi = R0 - 1, R0 - 1 + 24

    def coefficient(i, carry):
        mid = V[i + 1, lo:hi, :]
        around = [
            V[i + 2, lo:hi, :],
            V[i, lo:hi, :],
            V[i + 1, lo + 1:hi + 1, :],
            V[i + 1, lo - 1:hi - 1, :],
            pltpu.roll(mid, nz - 1, 1),
            pltpu.roll(mid, 1, 1),
        ]
        faces = [mid + a for a in around]
        total = faces[0]
        for f in faces[1:]:
            total = total + f
        recip = 1.0 / (1.0 + total)
        inv[i] = recip
        for k in range(6):
            C[k, i] = faces[k] * recip
        return carry

    lax.fori_loop(0, nx + 2, coefficient, 0)

    src[...] = jnp.zeros(src.shape, F32)
    for c in range(3):
        z = slice(c * nz, (c + 1) * nz)
        src[c, :, 1:2 + ny, :] = G[0:nx + 2, 0:ny + 1, z]
        src[c, :, 0:1, :] = G[0:nx + 2, YB - 1:YB, z]
    for c in gcopies:
        c.wait()
    for c in range(3):
        z = slice(c * nz, (c + 1) * nz)
        src[c, 0:3, 1:1 + ny, :] += gxp_rx[:, :, z]
        src[c, nx:nx + 2, 1:1 + ny, :] += gxm_rx[:, :, z]
        for k, (_, y) in enumerate(spread_reach(1, ny - 1)):
            src[c, 1:1 + nx, 1 + y, :] += gyp_rx[k, :, z]
        for k, (_, y) in enumerate(spread_reach(-1, ny - 1)):
            src[c, 1:1 + nx, 1 + y, :] += gym_rx[k, :, z]
        for i, d in enumerate(SIDES):
            for k, (_, _, x, y) in enumerate(spread_corner(d, nx, ny)):
                src[c, 1 + x, 1 + y:2 + y, :] += gc_rx[i, k, :, z]
        src[c] = src[c] * inv[...]

    def update(planes, low, high, colour):
        rows = high - low
        parity = (
            lax.broadcasted_iota(jnp.int32, (rows, nz), 0)
            + lax.broadcasted_iota(jnp.int32, (rows, nz), 1)
            + low
        ) % 2
        a, b = R0 + low, R0 + high
        p, q = 1 + low, 1 + high
        for x in planes:
            chosen = parity == (colour + x) % 2
            coef = [C[k, x + 1, p:q, :] for k in range(6)]
            for c in range(3):
                mid = S[c, x + 2, a:b, :]
                new = (
                    src[c, x + 1, p:q, :]
                    + coef[0] * S[c, x + 3, a:b, :]
                    + coef[1] * S[c, x + 1, a:b, :]
                    + coef[2] * S[c, x + 2, a + 1:b + 1, :]
                    + coef[3] * S[c, x + 2, a - 1:b - 1, :]
                    + coef[4] * pltpu.roll(mid, nz - 1, 1)
                    + coef[5] * pltpu.roll(mid, 1, 1)
                )
                S[c, x + 2, a:b, :] = jnp.where(chosen, new, mid)

    def sweep(r, carry):
        now, later = lax.rem(r, 2), lax.rem(r + 1, 2)
        edge = [0, 1, nx - 2, nx - 1]
        take_y(now)
        update(range(1, nx - 1), -1, 23, 0)
        take_x(now)
        update([-1, 0, nx - 1, nx], -1, 23, 0)
        update(edge, 0, ny, 1)

        @pl.when(r < SWEEPS - 1)
        def _():
            send_x(later)

        update(range(2, nx - 2), 0, ny, 1)

        @pl.when(r < SWEEPS - 1)
        def _():
            send_y(later)

        return carry

    lax.fori_loop(0, SWEEPS, sweep, 0)

    for c in range(3):
        flow[c] = S[c, 2:2 + nx, R0:R0 + ny, :]
        for k, (y, _) in enumerate(flow_reach(1, ny - 1)):
            fyp_tx[k, c] = S[c, 2:2 + nx, R0 + y, :]
        for k, (y, _) in enumerate(flow_reach(-1, ny - 1)):
            fym_tx[k, c] = S[c, 2:2 + nx, R0 + y, :]
        for i, d in enumerate(CORNERS):
            for k, (sx, sy, _, _) in enumerate(flow_corner(d, nx, ny)):
                fc_tx[i, 3 * k + c] = S[c, 2 + sx, R0 + sy:R0 + sy + 1, :]
    fcopies = [
        copy(flow.at[:, nx - 1:nx], fxp_rx, f_s.at[7], f_r.at[7], 7),
        copy(flow.at[:, 0:2], fxm_rx, f_s.at[1], f_r.at[1], 1),
        copy(fyp_tx, fyp_rx, f_s.at[5], f_r.at[5], 5),
        copy(fym_tx, fym_rx, f_s.at[3], f_r.at[3], 3),
    ]
    for i, d in enumerate(CORNERS):
        n = 3 * len(flow_corner(d, nx, ny))
        fcopies.append(copy(fc_tx.at[i, 0:n], fc_rx.at[i, 0:n], f_s.at[d], f_r.at[d], d))
    for c in fcopies:
        c.start()
    fld[...] = jnp.zeros(fld.shape, F32)
    for c in range(3):
        fld[c, 1:1 + nx, 0:ny, :] = S[c, 2:2 + nx, R0:R0 + ny, :]
    for c in fcopies:
        c.wait()
    fld[:, 0:1, 0:ny, :] = fxp_rx[...]
    fld[:, 1 + nx:3 + nx, 0:ny, :] = fxm_rx[...]
    for c in range(3):
        for k, (_, y) in enumerate(flow_reach(1, ny - 1)):
            fld[c, 1:1 + nx, g_row(y), :] = fyp_rx[k, c]
        for k, (_, y) in enumerate(flow_reach(-1, ny - 1)):
            fld[c, 1:1 + nx, g_row(y), :] = fym_rx[k, c]
        for i, d in enumerate(CORNERS):
            for k, (_, _, x, y) in enumerate(flow_corner(d, nx, ny)):
                fld[c, 1 + x, g_row(y):g_row(y) + 1, :] = fc_rx[i, 3 * k + c]
    high, low = split(fld[...].reshape(-1, nz))
    fld_hi[...] = high
    fld_lo[...] = low
    NN = (((1,), (0,)), ((), ()))

    def sample(d, carry):
        pairs = [tables(mk_rx[d, k]) for k in range(2)]
        txy = jnp.concatenate([p[0] for p in pairs], axis=1)
        tz_hi, tz_lo = split(jnp.concatenate([p[1] for p in pairs], axis=1))
        picked = dot(fld_hi[...], tz_hi, NN) + dot(fld_lo[...], tz_hi, NN) + dot(fld_hi[...], tz_lo, NN)
        rows = txy.shape[0]
        for c in range(3):
            total = jnp.sum(picked[c * rows:(c + 1) * rows] * txy, axis=0, keepdims=True)
            ret_tx[d, 0, c:c + 1] = total[:, :markers]
            ret_tx[d, 1, c:c + 1] = total[:, markers:]
        return carry

    ret_tx[...] = jnp.zeros(ret_tx.shape, F32)

    def give_back(d):
        return copy(ret_tx.at[d], ret_rx.at[d], ret_s.at[d], ret_r.at[d], d, -1)

    def sample_side(d, carry):
        sample(d, carry)
        give_back(d).start()
        return carry

    lax.fori_loop(0, 4, sample_side, 0)
    lax.fori_loop(5, 9, sample_side, 0)
    lax.fori_loop(4, 5, sample, 0)
    ret_rx[4] = ret_tx[4]
    for d in SIDES:
        give_back(d).wait()
    for b in range(blocks):
        mvel[b] = ret_rx[jnp.clip(going[b], 0, 8), jnp.clip(rank[b], 0, 1)][0:3]


def local(velocity, viscosity, marker_force, delta_weights, marker_cells, block_count, destination):
    nx, ny, nz = viscosity.shape
    size_x, size_y = lax.axis_size("gx"), lax.axis_size("gy")
    blocks, _, markers = marker_force.shape
    dma = pltpu.SemaphoreType.DMA
    vmem = pltpu.VMEM
    rows = 3 * (nx + 4) * YB
    scratch = [
        vmem((3, nx + 4, 40, nz), F32),
        vmem((nx + 4, 40, nz), F32),
        vmem((6, nx + 2, 24, nz), F32),
        vmem((nx + 2, 24, nz), F32),
        vmem((3, nx + 2, 24, nz), F32),
        vmem((nx + 4, YB, 3 * nz), F32),
        vmem((rows, nz), BF16),
        vmem((rows, nz), BF16),
        vmem((3, nx + 4, YB, nz), F32),
        vmem((blocks, 24, markers), F32),
        vmem((9, 2, 24, markers), F32), vmem((9, 2, 24, markers), F32), dma((9,)), dma((9,)),
        vmem((2, 2, ny, nz), F32),
        vmem((2, 2, nx, nz), F32), vmem((2, 2, nx, nz), F32),
        vmem((4, 1, nz), F32), vmem((4, 1, nz), F32), dma((9,)), dma((9,)),
        vmem((2, 2, 3, ny, nz), F32), vmem((2, 2, 3, ny, nz), F32),
        vmem((2, 2, 3, nx, nz), F32), vmem((2, 2, 3, nx, nz), F32),
        vmem((2, 4, 3, 1, nz), F32), vmem((2, 4, 3, 1, nz), F32), dma((2, 9)), dma((2, 9)),
        vmem((3, ny, 3 * nz), F32), vmem((2, ny, 3 * nz), F32),
        vmem((3, nx, 3 * nz), F32), vmem((3, nx, 3 * nz), F32),
        vmem((2, nx, 3 * nz), F32), vmem((2, nx, 3 * nz), F32),
        vmem((8, 8, 1, 3 * nz), F32), vmem((8, 8, 1, 3 * nz), F32), dma((17,)), dma((17,)),
        vmem((3, 1, ny, nz), F32), vmem((3, 2, ny, nz), F32),
        vmem((1, 3, nx, nz), F32), vmem((1, 3, nx, nz), F32),
        vmem((2, 3, nx, nz), F32), vmem((2, 3, nx, nz), F32),
        vmem((4, 12, 1, nz), F32), vmem((4, 12, 1, nz), F32), dma((9,)), dma((9,)),
        vmem((9, 2, 8, markers), F32), vmem((9, 2, 8, markers), F32), dma((9,)), dma((9,)),
    ]
    in_vmem = pl.BlockSpec(memory_space=pltpu.VMEM)
    in_smem = pl.BlockSpec(memory_space=pltpu.SMEM)
    return pl.pallas_call(
        functools.partial(kernel, size_x, size_y),
        out_shape=(
            jax.ShapeDtypeStruct(velocity.shape, F32),
            jax.ShapeDtypeStruct(marker_force.shape, F32),
        ),
        in_specs=[in_vmem] * 5 + [in_smem] * 2,
        out_specs=(in_vmem, in_vmem),
        scratch_shapes=scratch,
        compiler_params=pltpu.CompilerParams(
            collective_id=0, has_side_effects=True, vmem_limit_bytes=40 * 1024 * 1024
        ),
    )(velocity, viscosity, marker_force, delta_weights, marker_cells, block_count, destination)


def solution(mesh):
    return jax.shard_map(
        local,
        mesh=mesh,
        in_specs=(
            P(None, ("groups", "gx"), "gy", None),
            P(("groups", "gx"), "gy", None),
            P(("groups", "gx", "gy"), None, None),
            P(("groups", "gx", "gy"), None, None, None),
            P(("groups", "gx", "gy"), None, None),
            P(("groups", "gx", "gy")),
            P(("groups", "gx", "gy")),
        ),
        out_specs=(P(None, ("groups", "gx"), "gy", None), P(("groups", "gx", "gy"), None, None)),
        check_vma=False,
    )
```

```python
import functools

import jax
import jax.numpy as jnp
from jax import lax
from jax.experimental import pallas as pl
from jax.experimental.pallas import tpu as pltpu
from jax.sharding import PartitionSpec as P

SWEEPS = 8
MESH = pl.DeviceIdType.MESH
F32 = jnp.float32
BF16 = jnp.bfloat16
DIRS = [(dx, dy) for dx in (-1, 0, 1) for dy in (-1, 0, 1)]
SIDES = [d for d in range(9) if d != 4]
CORNERS = [0, 2, 6, 8]
YB = 24
R0 = 9
NT = (((1,), (1,)), ((), ()))


def split(value):
    scaled = value * 65537.0
    high = scaled - (scaled - value)
    return high.astype(BF16), (value - high).astype(BF16)


def spread_reach(step, last):
    if step == 0:
        return None
    if step > 0:
        return [(last, -1), (last + 1, 0), (last + 2, 1)]
    return [(-1, last), (0, last + 1)]


def flow_reach(step, last):
    if step > 0:
        return [(last, -1)]
    return [(0, last + 1), (1, last + 2)]


def spread_corner(d, nx, ny):
    dx, dy = DIRS[d]
    rows = []
    over_x = spread_reach(dx, nx - 1) or [(-1, -1), (nx, nx)]
    over_y = spread_reach(dy, ny - 1) or [(-1, -1), (ny, ny)]
    for sx, tx in over_x:
        for sy, ty in over_y:
            if not (tx in (-1, nx) and ty in (-1, ny)):
                rows.append((sx, sy, tx, ty))
    return rows


def flow_corner(d, nx, ny):
    dx, dy = DIRS[d]
    return [
        (sx, sy, tx, ty)
        for sx, tx in flow_reach(dx, nx - 1)
        for sy, ty in flow_reach(dy, ny - 1)
    ]


def kernel(
    size_x, size_y,
    vel, visc, force, weights, cells, count, dest,
    flow, mvel,
    S, V, C, inv, src, G, fld_hi, fld_lo, fld, packed,
    mk_tx, mk_rx, mk_s, mk_r,
    vx_rx, vy_tx, vy_rx, vc_tx, vc_rx, v_s, v_r,
    sx_tx, sx_rx, sy_tx, sy_rx, sc_tx, sc_rx, st_s, st_r,
    gxp_rx, gxm_rx, gyp_tx, gyp_rx, gym_tx, gym_rx, gc_tx, gc_rx, g_s, g_r,
    fxp_rx, fxm_rx, fyp_tx, fyp_rx, fym_tx, fym_rx, fc_tx, fc_rx, f_s, f_r,
    ret_tx, ret_rx, ret_s, ret_r,
):
    nx, ny, nz = visc.shape
    blocks, markers = force.shape[0], force.shape[2]
    here_x = lax.axis_index("gx")
    here_y = lax.axis_index("gy")

    def at(d, sign=1):
        dx, dy = DIRS[d] if isinstance(d, int) else (d // 3 - 1, d % 3 - 1)
        return {
            "gx": lax.rem(here_x + (sign * dx + size_x), size_x),
            "gy": lax.rem(here_y + (sign * dy + size_y), size_y),
        }

    def copy(a, b, s, r, d, sign=1):
        return pltpu.make_async_remote_copy(
            src_ref=a, dst_ref=b, send_sem=s, recv_sem=r,
            device_id=at(d, sign), device_id_type=MESH,
        )

    barrier = pltpu.get_barrier_semaphore()
    for d in SIDES:
        pl.semaphore_signal(barrier, inc=1, device_id=at(d), device_id_type=MESH)

    lane = lax.broadcasted_iota(jnp.int32, (1, markers), 1)
    for b in range(blocks):
        live = lane < count[b]
        packed[b, 0:3] = jnp.where(live, force[b], 0.0)
        for k in range(3):
            packed[b, 3 + 4 * k:7 + 4 * k] = jnp.where(live, weights[b, k], 0.0)
        packed[b, 15:18] = jnp.where(live, cells[b].astype(F32), 0.0)
        packed[b, 18:24] = jnp.zeros((6, markers), F32)
    going, rank = [], []
    for b in range(blocks):
        to = dest[b]
        step_x = lax.rem(lax.div(to, size_y) - here_x + (1 + size_x), size_x)
        step_y = lax.rem(lax.rem(to, size_y) - here_y + (1 + size_y), size_y)
        going.append(step_x * 3 + step_y)
        r = jnp.int32(0)
        for e in range(b):
            r = r + (going[e] == going[b]).astype(jnp.int32)
        rank.append(r)
    slot_of = [going[b] * 2 + rank[b] for b in range(blocks)]
    for d in range(9):
        for k in range(2):
            which, valid = jnp.int32(0), jnp.int32(0)
            for b in range(blocks):
                hit = (slot_of[b] == d * 2 + k).astype(jnp.int32)
                which, valid = which + b * hit, valid + hit
            block = packed[which] * valid.astype(F32)
            if d == 4:
                mk_rx[d, k] = block
            else:
                mk_tx[d, k] = block

    pl.semaphore_wait(barrier, 8)
    mk = {d: copy(mk_tx.at[d], mk_rx.at[d], mk_s.at[d], mk_r.at[d], d) for d in SIDES}
    for d in SIDES:
        mk[d].start()

    for i, lo in ((0, 0), (1, ny - 2)):
        for k in range(2):
            vy_tx[i, k] = visc[:, lo + k, :]
    for i, d in enumerate(CORNERS):
        dx, dy = DIRS[d]
        x, y = (nx - 1 if dx > 0 else 0), (ny - 1 if dy > 0 else 0)
        vc_tx[i] = visc[x, y:y + 1, :]
    vcopies = [
        copy(visc.at[0:2], vx_rx.at[0], v_s.at[1], v_r.at[1], 1),
        copy(visc.at[nx - 2:nx], vx_rx.at[1], v_s.at[7], v_r.at[7], 7),
        copy(vy_tx.at[0], vy_rx.at[0], v_s.at[3], v_r.at[3], 3),
        copy(vy_tx.at[1], vy_rx.at[1], v_s.at[5], v_r.at[5], 5),
    ] + [
        copy(vc_tx.at[i], vc_rx.at[i], v_s.at[d], v_r.at[d], d) for i, d in enumerate(CORNERS)
    ]
    for c in vcopies:
        c.start()

    S[...] = jnp.zeros(S.shape, F32)
    for c in range(3):
        S[c, 2:2 + nx, R0:R0 + ny, :] = vel[c]
    odd = (
        lax.broadcasted_iota(jnp.int32, (ny, nz), 0) + lax.broadcasted_iota(jnp.int32, (ny, nz), 1)
    ) % 2 == 1
    odd_x = (
        lax.broadcasted_iota(jnp.int32, (nx, nz), 0) + lax.broadcasted_iota(jnp.int32, (nx, nz), 1)
    ) % 2 == 1

    def corner_cell(d):
        dx, dy = DIRS[d]
        return (nx - 1 if dx > 0 else 0), (ny - 1 if dy > 0 else 0)

    def copies_x(slot):
        return [
            copy(sx_tx.at[slot, i], sx_rx.at[slot, i], st_s.at[slot, d], st_r.at[slot, d], d)
            for i, d in ((0, 1), (1, 7))
        ] + [
            copy(sc_tx.at[slot, i], sc_rx.at[slot, i], st_s.at[slot, d], st_r.at[slot, d], d)
            for i, d in enumerate(CORNERS)
        ]

    def copies_y(slot):
        return [
            copy(sy_tx.at[slot, i], sy_rx.at[slot, i], st_s.at[slot, d], st_r.at[slot, d], d)
            for i, d in ((0, 3), (1, 5))
        ]

    def send_x(slot):
        sends = copies_x(slot)
        for i, x in ((0, 0), (1, nx - 2)):
            for c in range(3):
                sx_tx[slot, i, c] = jnp.where(
                    odd, S[c, 2 + x, R0:R0 + ny, :], S[c, 3 + x, R0:R0 + ny, :]
                )
            sends[i].start()
        for i, d in enumerate(CORNERS):
            x, y = corner_cell(d)
            for c in range(3):
                sc_tx[slot, i, c] = S[c, 2 + x, R0 + y:R0 + y + 1, :]
            sends[2 + i].start()

    def send_y(slot):
        sends = copies_y(slot)
        for i, y in ((0, 0), (1, ny - 2)):
            for c in range(3):
                sy_tx[slot, i, c] = jnp.where(
                    odd_x, S[c, 2:2 + nx, R0 + y, :], S[c, 2:2 + nx, R0 + y + 1, :]
                )
            sends[i].start()

    def take_y(slot):
        for c in copies_y(slot):
            c.wait()
        for c in range(3):
            for i, y in ((0, ny), (1, -2)):
                tile = sy_rx[slot, i, c]
                S[c, 2:2 + nx, R0 + y, :] = tile
                S[c, 2:2 + nx, R0 + y + 1, :] = tile

    def take_x(slot):
        for c in copies_x(slot):
            c.wait()
        for c in range(3):
            for i, x in ((0, nx), (1, -2)):
                plane = sx_rx[slot, i, c]
                S[c, 2 + x, R0:R0 + ny, :] = plane
                S[c, 3 + x, R0:R0 + ny, :] = plane
            for i, d in enumerate(CORNERS):
                dx, dy = DIRS[d]
                x, y = (-1 if dx > 0 else nx), (-1 if dy > 0 else ny)
                S[c, 2 + x, R0 + y:R0 + y + 1, :] = sc_rx[slot, i, c]

    send_x(0)
    send_y(0)

    row_x = lax.broadcasted_iota(jnp.int32, (16, markers), 0)
    row_y = lax.broadcasted_iota(jnp.int32, (YB, markers), 0)
    row_z = lax.broadcasted_iota(jnp.int32, (nz, markers), 0)

    def tables(blk):
        place = blk[15:18].astype(jnp.int32)
        tx = jnp.zeros((16, markers), F32)
        ty = jnp.zeros((YB, markers), F32)
        tz = jnp.zeros((nz, markers), F32)
        for o in range(4):
            px = place[0:1] + o
            py = place[1:2] + (o - 1)
            py = jnp.where(py < 0, py + YB, py)
            pz = (place[2:3] + (o - 1 + nz)) % nz
            tx = jnp.where(row_x == px, blk[3 + o:4 + o], tx)
            ty = jnp.where(row_y == py, blk[7 + o:8 + o], ty)
            tz = jnp.where(row_z == pz, blk[11 + o:12 + o], tz)
        txy = jnp.concatenate([tx[i:i + 1] * ty for i in range(nx + 4)], axis=0)
        return txy, tz

    G[...] = jnp.zeros(G.shape, F32)
    for c in range(3):
        G[1:1 + nx, 0:ny, c * nz:(c + 1) * nz] = vel[c]
    def dot(a, b, dims):
        return lax.dot_general(a, b, dims, preferred_element_type=F32)

    def spread(d, carry):
        left, right = [], []
        for k in range(2):
            blk = mk_rx[d, k]
            txy, tz = tables(blk)
            left.append(txy)
            right.append(jnp.concatenate([tz * blk[c:c + 1] for c in range(3)], axis=0))
        left_hi, left_lo = split(jnp.concatenate(left, axis=1))
        right_hi, right_lo = split(jnp.concatenate(right, axis=1))
        got = dot(left_hi, right_hi, NT) + dot(left_hi, right_lo, NT) + dot(left_lo, right_hi, NT)
        G[...] += got.reshape(G.shape)
        return carry

    lax.fori_loop(4, 5, spread, 0)
    for d in SIDES:
        mk[d].wait()
    lax.fori_loop(0, 4, spread, 0)
    lax.fori_loop(5, 9, spread, 0)

    def g_row(y):
        return y % YB

    gcopies = [
        copy(G.at[nx:nx + 3, 0:ny], gxp_rx, g_s.at[7], g_r.at[7], 7),
        copy(G.at[0:2, 0:ny], gxm_rx, g_s.at[1], g_r.at[1], 1),
    ]
    for c in gcopies:
        c.start()
    for k, (y, _) in enumerate(spread_reach(1, ny - 1)):
        gyp_tx[k] = G[1:1 + nx, g_row(y), :]
    for k, (y, _) in enumerate(spread_reach(-1, ny - 1)):
        gym_tx[k] = G[1:1 + nx, g_row(y), :]
    for i, d in enumerate(SIDES):
        for k, (sx, sy, _, _) in enumerate(spread_corner(d, nx, ny)):
            gc_tx[i, k] = G[sx + 1, g_row(sy):g_row(sy) + 1, :]
    gcopies += [
        copy(gyp_tx, gyp_rx, g_s.at[5], g_r.at[5], 5),
        copy(gym_tx, gym_rx, g_s.at[3], g_r.at[3], 3),
    ]
    for i, d in enumerate(SIDES):
        n = len(spread_corner(d, nx, ny))
        gcopies.append(copy(gc_tx.at[i, 0:n], gc_rx.at[i, 0:n], g_s.at[9 + i], g_r.at[9 + i], d))
    for c in gcopies[2:]:
        c.start()
    V[...] = jnp.zeros(V.shape, F32)
    V[2:2 + nx, R0:R0 + ny, :] = visc[...]
    for c in vcopies:
        c.wait()
    for i, x in ((0, nx), (1, -2)):
        V[2 + x:4 + x, R0:R0 + ny, :] = vx_rx[i]
    for i, y in ((0, ny), (1, -2)):
        for k in range(2):
            V[2:2 + nx, R0 + y + k, :] = vy_rx[i, k]
    for i, d in enumerate(CORNERS):
        dx, dy = DIRS[d]
        x, y = (-1 if dx > 0 else nx), (-1 if dy > 0 else ny)
        V[2 + x, R0 + y:R0 + y + 1, :] = vc_rx[i]
    lo, hi = R0 - 1, R0 - 1 + 24

    def coefficient(i, carry):
        mid = V[i + 1, lo:hi, :]
        around = [
            V[i + 2, lo:hi, :],
            V[i, lo:hi, :],
            V[i + 1, lo + 1:hi + 1, :],
            V[i + 1, lo - 1:hi - 1, :],
            pltpu.roll(mid, nz - 1, 1),
            pltpu.roll(mid, 1, 1),
        ]
        faces = [mid + a for a in around]
        total = faces[0]
        for f in faces[1:]:
            total = total + f
        recip = 1.0 / (1.0 + total)
        inv[i] = recip
        for k in range(6):
            C[k, i] = faces[k] * recip
        return carry

    lax.fori_loop(0, nx + 2, coefficient, 0)

    src[...] = jnp.zeros(src.shape, F32)
    for c in range(3):
        z = slice(c * nz, (c + 1) * nz)
        src[c, :, 1:2 + ny, :] = G[0:nx + 2, 0:ny + 1, z]
        src[c, :, 0:1, :] = G[0:nx + 2, YB - 1:YB, z]
    for c in gcopies:
        c.wait()
    for c in range(3):
        z = slice(c * nz, (c + 1) * nz)
        src[c, 0:3, 1:1 + ny, :] += gxp_rx[:, :, z]
        src[c, nx:nx + 2, 1:1 + ny, :] += gxm_rx[:, :, z]
        for k, (_, y) in enumerate(spread_reach(1, ny - 1)):
            src[c, 1:1 + nx, 1 + y, :] += gyp_rx[k, :, z]
        for k, (_, y) in enumerate(spread_reach(-1, ny - 1)):
            src[c, 1:1 + nx, 1 + y, :] += gym_rx[k, :, z]
        for i, d in enumerate(SIDES):
            for k, (_, _, x, y) in enumerate(spread_corner(d, nx, ny)):
                src[c, 1 + x, 1 + y:2 + y, :] += gc_rx[i, k, :, z]
        src[c] = src[c] * inv[...]

    def update(planes, low, high, colour):
        rows = high - low
        parity = (
            lax.broadcasted_iota(jnp.int32, (rows, nz), 0)
            + lax.broadcasted_iota(jnp.int32, (rows, nz), 1)
            + low
        ) % 2
        a, b = R0 + low, R0 + high
        p, q = 1 + low, 1 + high
        for x in planes:
            chosen = parity == (colour + x) % 2
            coef = [C[k, x + 1, p:q, :] for k in range(6)]
            for c in range(3):
                mid = S[c, x + 2, a:b, :]
                new = (
                    src[c, x + 1, p:q, :]
                    + coef[0] * S[c, x + 3, a:b, :]
                    + coef[1] * S[c, x + 1, a:b, :]
                    + coef[2] * S[c, x + 2, a + 1:b + 1, :]
                    + coef[3] * S[c, x + 2, a - 1:b - 1, :]
                    + coef[4] * pltpu.roll(mid, nz - 1, 1)
                    + coef[5] * pltpu.roll(mid, 1, 1)
                )
                S[c, x + 2, a:b, :] = jnp.where(chosen, new, mid)

    def sweep(r, carry):
        now, later = lax.rem(r, 2), lax.rem(r + 1, 2)
        edge = [0, 1, nx - 2, nx - 1]
        take_y(now)
        update(range(1, nx - 1), -1, 23, 0)
        take_x(now)
        update([-1, 0, nx - 1, nx], -1, 23, 0)
        update(edge, 0, ny, 1)

        @pl.when(r < SWEEPS - 1)
        def _():
            send_x(later)

        update(range(2, nx - 2), 0, ny, 1)

        @pl.when(r < SWEEPS - 1)
        def _():
            send_y(later)

        return carry

    lax.fori_loop(0, SWEEPS, sweep, 0)

    for c in range(3):
        flow[c] = S[c, 2:2 + nx, R0:R0 + ny, :]
    fcopies = [
        copy(flow.at[:, nx - 1:nx], fxp_rx, f_s.at[7], f_r.at[7], 7),
        copy(flow.at[:, 0:2], fxm_rx, f_s.at[1], f_r.at[1], 1),
    ]
    for c in fcopies:
        c.start()
    for c in range(3):
        for k, (y, _) in enumerate(flow_reach(1, ny - 1)):
            fyp_tx[k, c] = S[c, 2:2 + nx, R0 + y, :]
        for k, (y, _) in enumerate(flow_reach(-1, ny - 1)):
            fym_tx[k, c] = S[c, 2:2 + nx, R0 + y, :]
        for i, d in enumerate(CORNERS):
            for k, (sx, sy, _, _) in enumerate(flow_corner(d, nx, ny)):
                fc_tx[i, 3 * k + c] = S[c, 2 + sx, R0 + sy:R0 + sy + 1, :]
    fcopies += [
        copy(fyp_tx, fyp_rx, f_s.at[5], f_r.at[5], 5),
        copy(fym_tx, fym_rx, f_s.at[3], f_r.at[3], 3),
    ]
    for i, d in enumerate(CORNERS):
        n = 3 * len(flow_corner(d, nx, ny))
        fcopies.append(copy(fc_tx.at[i, 0:n], fc_rx.at[i, 0:n], f_s.at[d], f_r.at[d], d))
    for c in fcopies[2:]:
        c.start()
    fld[...] = jnp.zeros(fld.shape, F32)
    for c in range(3):
        fld[c, 1:1 + nx, 0:ny, :] = S[c, 2:2 + nx, R0:R0 + ny, :]
    for c in fcopies:
        c.wait()
    fld[:, 0:1, 0:ny, :] = fxp_rx[...]
    fld[:, 1 + nx:3 + nx, 0:ny, :] = fxm_rx[...]
    for c in range(3):
        for k, (_, y) in enumerate(flow_reach(1, ny - 1)):
            fld[c, 1:1 + nx, g_row(y), :] = fyp_rx[k, c]
        for k, (_, y) in enumerate(flow_reach(-1, ny - 1)):
            fld[c, 1:1 + nx, g_row(y), :] = fym_rx[k, c]
        for i, d in enumerate(CORNERS):
            for k, (_, _, x, y) in enumerate(flow_corner(d, nx, ny)):
                fld[c, 1 + x, g_row(y):g_row(y) + 1, :] = fc_rx[i, 3 * k + c]
    high, low = split(fld[...].reshape(-1, nz))
    fld_hi[...] = high
    fld_lo[...] = low
    NN = (((1,), (0,)), ((), ()))

    def sample(d, carry):
        pairs = [tables(mk_rx[d, k]) for k in range(2)]
        txy = jnp.concatenate([p[0] for p in pairs], axis=1)
        tz_hi, tz_lo = split(jnp.concatenate([p[1] for p in pairs], axis=1))
        picked = dot(fld_hi[...], tz_hi, NN) + dot(fld_lo[...], tz_hi, NN) + dot(fld_hi[...], tz_lo, NN)
        rows = txy.shape[0]
        for c in range(3):
            total = jnp.sum(picked[c * rows:(c + 1) * rows] * txy, axis=0, keepdims=True)
            ret_tx[d, 0, c:c + 1] = total[:, :markers]
            ret_tx[d, 1, c:c + 1] = total[:, markers:]
        return carry

    ret_tx[...] = jnp.zeros(ret_tx.shape, F32)

    def give_back(d):
        return copy(ret_tx.at[d], ret_rx.at[d], ret_s.at[d], ret_r.at[d], d, -1)

    def sample_side(d, carry):
        sample(d, carry)
        give_back(d).start()
        return carry

    lax.fori_loop(0, 4, sample_side, 0)
    lax.fori_loop(5, 9, sample_side, 0)
    lax.fori_loop(4, 5, sample, 0)
    ret_rx[4] = ret_tx[4]
    for d in SIDES:
        give_back(d).wait()
    for b in range(blocks):
        mvel[b] = ret_rx[jnp.clip(going[b], 0, 8), jnp.clip(rank[b], 0, 1)][0:3]


def local(velocity, viscosity, marker_force, delta_weights, marker_cells, block_count, destination):
    nx, ny, nz = viscosity.shape
    size_x, size_y = lax.axis_size("gx"), lax.axis_size("gy")
    blocks, _, markers = marker_force.shape
    dma = pltpu.SemaphoreType.DMA
    vmem = pltpu.VMEM
    rows = 3 * (nx + 4) * YB
    scratch = [
        vmem((3, nx + 4, 40, nz), F32),
        vmem((nx + 4, 40, nz), F32),
        vmem((6, nx + 2, 24, nz), F32),
        vmem((nx + 2, 24, nz), F32),
        vmem((3, nx + 2, 24, nz), F32),
        vmem((nx + 4, YB, 3 * nz), F32),
        vmem((rows, nz), BF16),
        vmem((rows, nz), BF16),
        vmem((3, nx + 4, YB, nz), F32),
        vmem((blocks, 24, markers), F32),
        vmem((9, 2, 24, markers), F32), vmem((9, 2, 24, markers), F32), dma((9,)), dma((9,)),
        vmem((2, 2, ny, nz), F32),
        vmem((2, 2, nx, nz), F32), vmem((2, 2, nx, nz), F32),
        vmem((4, 1, nz), F32), vmem((4, 1, nz), F32), dma((9,)), dma((9,)),
        vmem((2, 2, 3, ny, nz), F32), vmem((2, 2, 3, ny, nz), F32),
        vmem((2, 2, 3, nx, nz), F32), vmem((2, 2, 3, nx, nz), F32),
        vmem((2, 4, 3, 1, nz), F32), vmem((2, 4, 3, 1, nz), F32), dma((2, 9)), dma((2, 9)),
        vmem((3, ny, 3 * nz), F32), vmem((2, ny, 3 * nz), F32),
        vmem((3, nx, 3 * nz), F32), vmem((3, nx, 3 * nz), F32),
        vmem((2, nx, 3 * nz), F32), vmem((2, nx, 3 * nz), F32),
        vmem((8, 8, 1, 3 * nz), F32), vmem((8, 8, 1, 3 * nz), F32), dma((17,)), dma((17,)),
        vmem((3, 1, ny, nz), F32), vmem((3, 2, ny, nz), F32),
        vmem((1, 3, nx, nz), F32), vmem((1, 3, nx, nz), F32),
        vmem((2, 3, nx, nz), F32), vmem((2, 3, nx, nz), F32),
        vmem((4, 12, 1, nz), F32), vmem((4, 12, 1, nz), F32), dma((9,)), dma((9,)),
        vmem((9, 2, 8, markers), F32), vmem((9, 2, 8, markers), F32), dma((9,)), dma((9,)),
    ]
    in_vmem = pl.BlockSpec(memory_space=pltpu.VMEM)
    in_smem = pl.BlockSpec(memory_space=pltpu.SMEM)
    return pl.pallas_call(
        functools.partial(kernel, size_x, size_y),
        out_shape=(
            jax.ShapeDtypeStruct(velocity.shape, F32),
            jax.ShapeDtypeStruct(marker_force.shape, F32),
        ),
        in_specs=[in_vmem] * 5 + [in_smem] * 2,
        out_specs=(in_vmem, in_vmem),
        scratch_shapes=scratch,
        compiler_params=pltpu.CompilerParams(
            collective_id=0, has_side_effects=True, vmem_limit_bytes=40 * 1024 * 1024
        ),
    )(velocity, viscosity, marker_force, delta_weights, marker_cells, block_count, destination)


def solution(mesh):
    return jax.shard_map(
        local,
        mesh=mesh,
        in_specs=(
            P(None, ("groups", "gx"), "gy", None),
            P(("groups", "gx"), "gy", None),
            P(("groups", "gx", "gy"), None, None),
            P(("groups", "gx", "gy"), None, None, None),
            P(("groups", "gx", "gy"), None, None),
            P(("groups", "gx", "gy")),
            P(("groups", "gx", "gy")),
        ),
        out_specs=(P(None, ("groups", "gx"), "gy", None), P(("groups", "gx", "gy"), None, None)),
        check_vma=False,
    )
```
